32 devices in a mesh: dp: 8 (over y, x, core), tensor: 4 (over z).
Axes of the slice: x: 2, y: 2, z: 4, core: 2. Of those that a mesh axis runs over, the one named last changes fastest.
Arguments:
- tokens: bfloat16 [4096, 8192], P('dp'), may hold values from -40 to 40
- cotangent: bfloat16 [4096, 2048], P('dp', 'tensor'), may hold values from -260 to 260
- master: float32 [8200, 2048], P('dp', 'tensor'), may hold values from -0.0625 to 0.0625
- first_moment: float32 [8200, 2048], P('dp', 'tensor'), may hold values from -0.0014648438 to 0.0014648438
- second_moment: float32 [8200, 2048], P('dp', 'tensor'), may hold values from 1.7881393e-09 to 1.7881393e-07
- old_rows: int32 [8200], P('dp'), may hold values from 0 to 8199, as said below
Outputs:
- keys_values: bfloat16 [4096, 2048], P('dp', 'tensor')
- update: float32 [8200, 2048], P('dp', 'tensor')
The draws below stay inside these ranges and needn't reach their ends.
Inputs may be any that keep to these rules, and one draw needn't show every extreme that they name: `old_rows`: every row 0 to 8199 is named by exactly one slot. Rows j * 1025 to (j + 1) * 1025 - 1 belong to new owner j; the slots of one device name at most 257 rows of one owner.
All inputs are finite; a program needn't handle non-finite values.
Results may differ from the reference program's by a relative error of at most 0.0049.
Values may be sent and summed in bfloat16 or wider, within the bound.
A program may use at most 128 MiB of HBM per device.

```python
import math
import jax
import jax.numpy as jnp

D = 8192
TOK_DEV = 512
KVC = 2048
ROWS_DEV = 1025
ROWS = 8200
TOKENS = 4096


def mixed_noise(key, rows, width):
    first, third = jax.random.split(key, 2)
    blocks = rows // TOK_DEV
    noise = jax.random.truncated_normal(first, -6.0, 6.0, (blocks, TOK_DEV, width), jnp.float32)
    local = jax.random.truncated_normal(third, -4.0, 4.0, (blocks, 1, width), jnp.float32)
    mixed = 0.937 * noise + 0.35 * local
    return mixed.reshape(rows, width)


def draw_tokens(key, part):
    base = jax.random.fold_in(key, 101)
    first, second = jax.random.split(base)
    noise = mixed_noise(first, TOKENS, D)
    ramp = jnp.arange(D, dtype=jnp.float32) / (D - 1)
    column = 3.0 ** ramp
    row = 0.35 * 3.0 ** jax.random.uniform(second, (TOKENS, 1), jnp.float32)
    return (noise * column[None, :] * row).astype(jnp.bfloat16)


def draw_cotangent(key, part):
    base = jax.random.fold_in(key, 202)
    first, second = jax.random.split(base)
    noise = mixed_noise(first, TOKENS, KVC)
    column = 3.0 ** (jnp.arange(KVC, dtype=jnp.float32) / (KVC - 1))
    row = 10.0 ** jax.random.uniform(second, (TOKENS, 1), jnp.float32)
    return (noise * column[None, :] * row).astype(jnp.bfloat16)


def draw_old_rows(key, part):
    rows_dev = ROWS_DEV
    peers = ROWS // ROWS_DEV
    base = jax.random.fold_in(key, 303)
    key_split, key_offset, key_order, key_slots = jax.random.split(base, 4)
    whole = rows_dev // peers
    spare = rows_dev % peers
    halves = peers // 2
    pair_ids = jnp.arange(halves, dtype=jnp.int32)
    extra = jnp.clip(spare - 2 * pair_ids, 0, 2)
    pair_total = 2 * whole + extra
    first_size = jax.random.randint(key_split, (halves,), 0, pair_total + 1)
    first_size = jnp.where(pair_ids == 0, pair_total, first_size)
    sizes = jnp.stack([first_size, pair_total - first_size], axis=1).reshape(peers).astype(jnp.int32)
    prefix = (jnp.cumsum(sizes) - sizes).astype(jnp.int32)
    offsets = jax.random.permutation(key_offset, peers).astype(jnp.int32)
    order = jax.random.permutation(key_order, peers).astype(jnp.int32)
    order_back = jnp.argsort(order).astype(jnp.int32)
    class_sorted = jnp.repeat(jnp.arange(peers, dtype=jnp.int32), sizes, total_repeat_length=rows_dev)
    rank_sorted = jnp.arange(rows_dev, dtype=jnp.int32) - prefix[class_sorted]

    def one_device(device):
        shuffle = jax.random.permutation(jax.random.fold_in(key_slots, device), rows_dev)
        classes = class_sorted[shuffle]
        ranks = rank_sorted[shuffle]
        owners = order[(order_back[device] + offsets[classes]) % peers]
        return owners * rows_dev + prefix[classes] + ranks
    table = jax.vmap(one_device)(jnp.arange(peers, dtype=jnp.int32))
    return table.reshape(peers * rows_dev).astype(jnp.int32)


def level_of(key, extent, cuts, low, top_value):
    gain = 1.0
    for position, blocks in cuts:
        steps = jax.random.uniform(jax.random.fold_in(jax.random.fold_in(key, 6), position), (blocks,), jnp.float32, low / len(cuts), top_value / len(cuts))
        gain = gain * jnp.repeat(jnp.exp(steps), extent[position] // blocks).reshape((-1,) + (1,) * (len(extent) - 1 - position))
    return gain


def gaussian(key, dims, deviation, reach, shards=(), kind=jnp.bfloat16):
    array = jax.random.normal(key, dims, jnp.float32) * deviation
    if len(shards) > 0:
        array = level_of(key, dims, shards, -0.22, 0.18) * array
    return jnp.clip(array, min=-reach, max=reach).astype(kind)


def setup_inputs(seed: int = 0) -> dict:
    splits = jax.random.split(jax.random.key(seed), 7)
    return {
        "tokens": draw_tokens(jax.random.fold_in(splits[6], 71), 0),
        "cotangent": draw_cotangent(jax.random.fold_in(splits[6], 71), 0),
        "master": gaussian(splits[2], (ROWS, KVC), D ** -0.5, 0.0625, ((0, 8), (1, 4)), jnp.float32),
        "first_moment": gaussian(splits[3], (ROWS, KVC), (1.0 / (D * KVC) ** 0.5), 0.0014648438, ((0, 8), (1, 4)), jnp.float32),
        "second_moment": jnp.clip(jnp.exp(math.log(1.7881393432617188e-07) - 4.6051702 * jax.random.uniform(splits[4], (ROWS, KVC), jnp.float32) ** level_of(splits[4], (ROWS, KVC), ((0, 8), (1, 4)), -0.2, 0.2)), 1.7881393032936899e-09, 1.7881393432617188e-07),
        "old_rows": draw_old_rows(jax.random.fold_in(splits[6], 71), 0),
    }


beta_one = 0.9
beta_two = 0.95
adam_eps = 1e-08
clip_norm = 1.0

def reference(tokens, cotangent, master, first_moment, second_moment, old_rows):
    new_master = jnp.zeros_like(master).at[old_rows].set(master)
    new_first = jnp.zeros_like(first_moment).at[old_rows].set(first_moment)
    new_second = jnp.zeros_like(second_moment).at[old_rows].set(second_moment)
    weight = new_master[:D].astype(jnp.bfloat16)
    keys_values = jnp.dot(tokens, weight, preferred_element_type=jnp.float32).astype(jnp.bfloat16)
    gradient = jnp.dot(tokens.T, cotangent, preferred_element_type=jnp.float32)
    gradient = jnp.concatenate([gradient, jnp.zeros((ROWS - D, KVC), jnp.float32)], axis=0)
    squares = jnp.sum(gradient * gradient)
    factor = clip_norm / (jnp.sqrt(squares) + 1e-06)
    clipped = gradient * factor
    moment_one = beta_one * new_first + (1.0 - beta_one) * clipped
    moment_two = beta_two * new_second + (1.0 - beta_two) * clipped * clipped
    update = moment_one / (jnp.sqrt(moment_two) + adam_eps)
    return (keys_values, update)
```

```python
import jax
import jax.numpy as jnp
from jax import lax
from jax.sharding import PartitionSpec as P

beta_one = 0.9
beta_two = 0.95
adam_eps = 1e-08
clip_norm = 1.0


def chip_partner(chips, step):
    if chips & (chips - 1) == 0:
        return [c ^ step for c in range(chips)]
    return [(c + step) % chips for c in range(chips)]


def reduce_scatter(partial, rows_dev, peers):
    chips = peers // 2
    me = lax.axis_index("dp")
    core, chip = me % 2, me // 2
    swap = [(d, d ^ 1) for d in range(peers)]
    total = None
    arrived = []
    for step in list(range(chips - 1, 0, -1)) + [0]:
        goes = chip_partner(chips, step)
        target = chip ^ step if chips & (chips - 1) == 0 else (chip + step) % chips
        other = lax.dynamic_slice_in_dim(partial, (2 * target + 1 - core) * rows_dev, rows_dev, 0)
        mine = lax.dynamic_slice_in_dim(partial, (2 * target + core) * rows_dev, rows_dev, 0)
        got = lax.ppermute(other, "dp", swap)
        both = mine.astype(jnp.float32) + got.astype(jnp.float32)
        if step == 0:
            total = both
        else:
            route = [(2 * c + k, 2 * goes[c] + k) for c in range(chips) for k in range(2)]
            arrived.append(lax.ppermute(both.astype(jnp.bfloat16), "dp", route))
    for block in arrived:
        total = total + block.astype(jnp.float32)
    return total


def per_device(tokens, cotangent, master, first_moment, second_moment, old_rows):
    rows_dev = master.shape[0]
    columns_dev = master.shape[1]
    peers = lax.axis_size("dp")
    features = tokens.shape[1]
    all_rows = rows_dev * peers
    capacity = 2 * (rows_dev // peers) + min(rows_dev % peers, 2)
    capacity = -(-capacity // 16) * 16
    owners = old_rows // rows_dev
    targets = old_rows % rows_dev
    chosen = (owners[:, None] == jnp.arange(peers, dtype=jnp.int32)[None, :]).astype(jnp.int32)
    within = jnp.sum((jnp.cumsum(chosen, axis=0) - 1) * chosen, axis=1)
    places = owners * capacity + within
    saved_weight, saved_map = (
        lax.all_gather(master.astype(jnp.bfloat16), "dp", axis=0, tiled=True),
        lax.all_gather(old_rows, "dp", axis=0, tiled=True),
    )

    whole = lax.dot_general(
        tokens, cotangent, (((0,), (0,)), ((), ())), preferred_element_type=jnp.float32
    ).astype(jnp.bfloat16)
    whole = jnp.pad(whole, ((0, all_rows - features), (0, 0)))
    gradient = reduce_scatter(whole, rows_dev, peers)

    box = jnp.arange(peers * capacity, dtype=jnp.int32)
    picks = box[:, None] == places[None, :]
    moments = jnp.concatenate(
        [first_moment.astype(jnp.bfloat16), second_moment.astype(jnp.bfloat16)], axis=1
    )
    outbox = jnp.dot(
        picks.astype(jnp.bfloat16), moments, preferred_element_type=jnp.float32
    ).astype(jnp.bfloat16)
    labels = jnp.max(jnp.where(picks, targets[None, :] + 1, 0), axis=1) - 1
    arrived = lax.all_to_all(
        outbox.reshape(peers, capacity, 2 * columns_dev), "dp", 0, 0, tiled=True
    ).reshape(peers * capacity, 2 * columns_dev)
    arrived_labels = lax.all_to_all(
        labels.reshape(peers, capacity), "dp", 0, 0, tiled=True
    ).reshape(-1)
    puts = jnp.arange(rows_dev, dtype=jnp.int32)[:, None] == arrived_labels[None, :]
    placed = jnp.dot(puts.astype(jnp.bfloat16), arrived, preferred_element_type=jnp.float32)

    weight_full = jnp.zeros((all_rows, columns_dev), jnp.bfloat16).at[saved_map].set(
        saved_weight, unique_indices=True
    )
    product = jnp.dot(tokens, weight_full[:features], preferred_element_type=jnp.float32)
    keys_values = product.astype(jnp.bfloat16)

    squares = lax.psum(jnp.sum(gradient * gradient), ("dp", "tensor"))
    factor = clip_norm / (jnp.sqrt(squares) + 1e-06)
    clipped = gradient * factor
    moment_one = beta_one * placed[:, :columns_dev] + (1.0 - beta_one) * clipped
    moment_two = beta_two * placed[:, columns_dev:] + (1.0 - beta_two) * clipped * clipped
    update = moment_one / (jnp.sqrt(moment_two) + adam_eps)
    return (keys_values, update)


def solution(mesh):
    in_specs = (
        P("dp", None),
        P("dp", "tensor"),
        P("dp", "tensor"),
        P("dp", "tensor"),
        P("dp", "tensor"),
        P("dp"),
    )
    out_specs = (P("dp", "tensor"), P("dp", "tensor"))
    return jax.shard_map(
        per_device, mesh=mesh, in_specs=in_specs, out_specs=out_specs, check_vma=False
    )
```

```python
import functools

import jax
import jax.numpy as jnp
from jax import lax
from jax.experimental import pallas as pl
from jax.experimental.pallas import tpu as pltpu
from jax.sharding import PartitionSpec as P

beta_one = 0.9
beta_two = 0.95
adam_eps = 1e-08
clip_norm = 1.0


def chip_partner(chips, step):
    if chips & (chips - 1) == 0:
        return [c ^ step for c in range(chips)]
    return [(c + step) % chips for c in range(chips)]


def sum_kernel(peers, groups, x_ref, o_ref, part, from_dp, from_tensor, send_dp, recv_dp, send_t, recv_t):
    row = lax.axis_index("dp")
    column = lax.axis_index("tensor")
    rows = [lax.rem(row + s, peers) for s in range(1, peers)]
    columns = [lax.rem(column + s, groups) for s in range(1, groups)]
    everyone = [(r, column) for r in rows] + [(row, c) for c in columns]
    barrier = pltpu.get_barrier_semaphore()
    for device in everyone:
        pl.semaphore_signal(barrier, inc=1, device_id=device, device_id_type=pl.DeviceIdType.MESH)
    pl.semaphore_wait(barrier, len(everyone))

    def exchange(source, slots, send, recv, devices):
        copies = [
            pltpu.make_async_remote_copy(
                src_ref=source,
                dst_ref=slots.at[k],
                send_sem=send.at[k],
                recv_sem=recv.at[k],
                device_id=device,
                device_id_type=pl.DeviceIdType.MESH,
            )
            for k, device in enumerate(devices)
        ]
        for copy in copies:
            copy.start()
        for copy in copies:
            copy.wait()
        total = source[...]
        for k in range(len(devices)):
            total = total + slots[k]
        return total

    part[...] = exchange(x_ref, from_dp, send_dp, recv_dp, [(r, column) for r in rows])
    o_ref[...] = exchange(part, from_tensor, send_t, recv_t, [(row, c) for c in columns])


def sum_over_mesh(value):
    peers, groups = lax.axis_size("dp"), lax.axis_size("tensor")
    tile = (8, 128)
    return pl.pallas_call(
        functools.partial(sum_kernel, peers, groups),
        out_shape=jax.ShapeDtypeStruct(tile, jnp.float32),
        in_specs=[pl.BlockSpec(memory_space=pltpu.VMEM)],
        out_specs=pl.BlockSpec(memory_space=pltpu.VMEM),
        scratch_shapes=[
            pltpu.VMEM(tile, jnp.float32),
            pltpu.VMEM((peers - 1,) + tile, jnp.float32),
            pltpu.VMEM((groups - 1,) + tile, jnp.float32),
            pltpu.SemaphoreType.DMA((peers - 1,)),
            pltpu.SemaphoreType.DMA((peers - 1,)),
            pltpu.SemaphoreType.DMA((groups - 1,)),
            pltpu.SemaphoreType.DMA((groups - 1,)),
        ],
        compiler_params=pltpu.CompilerParams(collective_id=0, has_side_effects=True),
    )(jnp.full(tile, value, jnp.float32))[0, 0]


def sum_cores(partial, rows_dev, peers):
    chips = peers // 2
    me = lax.axis_index("dp")
    core, chip = me % 2, me // 2
    swap = [(d, d ^ 1) for d in range(peers)]
    sums = []
    for step in range(chips):
        target = chip ^ step if chips & (chips - 1) == 0 else (chip + step) % chips
        other = lax.dynamic_slice_in_dim(partial, (2 * target + 1 - core) * rows_dev, rows_dev, 0)
        mine = lax.dynamic_slice_in_dim(partial, (2 * target + core) * rows_dev, rows_dev, 0)
        got = lax.ppermute(other, "dp", swap)
        both = mine.astype(jnp.float32) + got.astype(jnp.float32)
        sums.append(both if step == 0 else both.astype(jnp.bfloat16))
    return sums


def sum_chips(own, blocks, peers):
    chips = peers // 2
    arrived = []
    for step, block in reversed(list(enumerate(blocks, 1))):
        goes = chip_partner(chips, step)
        route = [(2 * c + k, 2 * goes[c] + k) for c in range(chips) for k in range(2)]
        arrived.append(lax.ppermute(block, "dp", route))
    for block in arrived:
        own = own + block.astype(jnp.float32)
    return own


def per_device(tokens, cotangent, master, first_moment, second_moment, old_rows):
    rows_dev = master.shape[0]
    columns_dev = master.shape[1]
    peers = lax.axis_size("dp")
    features = tokens.shape[1]
    all_rows = rows_dev * peers
    capacity = 2 * (rows_dev // peers) + min(rows_dev % peers, 2)
    capacity = -(-capacity // 16) * 16
    owners = old_rows // rows_dev
    targets = old_rows % rows_dev
    chosen = (owners[:, None] == jnp.arange(peers, dtype=jnp.int32)[None, :]).astype(jnp.int32)
    within = jnp.sum((jnp.cumsum(chosen, axis=0) - 1) * chosen, axis=1)
    places = owners * capacity + within

    box = jnp.arange(peers * capacity, dtype=jnp.int32)
    picks = box[:, None] == places[None, :]
    labels = jnp.max(jnp.where(picks, targets[None, :] + 1, 0), axis=1) - 1
    notes = jnp.concatenate(
        [
            labels.reshape(peers, 1, capacity),
            jnp.broadcast_to(old_rows[None, None, :], (peers, 1, rows_dev)),
        ],
        axis=2,
    )
    notes = lax.all_to_all(notes, "dp", 0, 0, tiled=True)
    arrived_labels = notes[:, 0, :capacity].reshape(-1)
    saved_map = notes[:, 0, capacity:].reshape(-1)
    saved_weight = lax.all_gather(master.astype(jnp.bfloat16), "dp", axis=0, tiled=True)

    whole = lax.dot_general(
        tokens, cotangent, (((0,), (0,)), ((), ())), preferred_element_type=jnp.float32
    ).astype(jnp.bfloat16)
    whole = jnp.pad(whole, ((0, all_rows - features), (0, 0)))
    own, *blocks = sum_cores(whole, rows_dev, peers)
    moments = jnp.concatenate(
        [first_moment.astype(jnp.bfloat16), second_moment.astype(jnp.bfloat16)], axis=1
    )
    outbox = jnp.dot(
        picks.astype(jnp.bfloat16), moments, preferred_element_type=jnp.float32
    ).astype(jnp.bfloat16)
    saved_weight, outbox, blocks = lax.optimization_barrier((saved_weight, outbox, blocks))
    gradient = sum_chips(own, blocks, peers)
    arrived = lax.all_to_all(
        outbox.reshape(peers, capacity, 2 * columns_dev), "dp", 0, 0, tiled=True
    ).reshape(peers * capacity, 2 * columns_dev)
    puts = jnp.arange(rows_dev, dtype=jnp.int32)[:, None] == arrived_labels[None, :]
    placed = jnp.dot(puts.astype(jnp.bfloat16), arrived, preferred_element_type=jnp.float32)

    weight_full = jnp.zeros((all_rows, columns_dev), jnp.bfloat16).at[saved_map].set(
        saved_weight, unique_indices=True
    )
    product = jnp.dot(tokens, weight_full[:features], preferred_element_type=jnp.float32)
    keys_values = product.astype(jnp.bfloat16)

    local, keys_values = lax.optimization_barrier((jnp.sum(gradient * gradient), keys_values))
    squares = sum_over_mesh(local)
    factor = clip_norm / (jnp.sqrt(squares) + 1e-06)
    clipped = gradient * factor
    moment_one = beta_one * placed[:, :columns_dev] + (1.0 - beta_one) * clipped
    moment_two = beta_two * placed[:, columns_dev:] + (1.0 - beta_two) * clipped * clipped
    update = moment_one / (jnp.sqrt(moment_two) + adam_eps)
    return (keys_values, update)


def solution(mesh):
    in_specs = (
        P("dp", None),
        P("dp", "tensor"),
        P("dp", "tensor"),
        P("dp", "tensor"),
        P("dp", "tensor"),
        P("dp"),
    )
    out_specs = (P("dp", "tensor"), P("dp", "tensor"))
    return jax.shard_map(
        per_device, mesh=mesh, in_specs=in_specs, out_specs=out_specs, check_vma=False
    )
```
